32 devices in a mesh: lat: 4 (over z), lon: 8 (over y, x, core).
Axes of the slice: x: 2, y: 2, z: 4, core: 2. Of those that a mesh axis runs over, the one named last changes fastest.
Arguments:
- control: float32 [4, 90, 32, 1024], P(None, None, 'lat', 'lon'), may hold values from -6 to 6
- kappa: float32 [4, 90, 32, 1024], P(None, None, 'lat', 'lon'), may hold values from 0.25 to 0.5
- pc_obs: bfloat16 [1024, 128, 300], P(('lat', 'lon')), may hold values from -6 to 6
- owner: int32 [1024, 1], P(('lat', 'lon')), may hold values from 0 to 31; in each aligned block of 32 rows (0 to 31, 32 to 63, ...) at most 2 rows name the same one
- columns: int32 [1024, 128], P(('lat', 'lon')), may hold values from 0 to 1023
- counts: int32 [1024], P(('lat', 'lon')), may hold values from 1 to 128, as said below
- jacobian: bfloat16 [360, 300], replicated, may hold values from -0.3125 to 0.3125
- obs_weight: float32 [300], replicated, may hold values from 0.3 to 3
Outputs:
- gradient: float32 [4, 90, 32, 1024], P(None, None, 'lat', 'lon')
The draws below stay inside these ranges and needn't reach their ends.
Inputs may be any that keep to these rules, and one draw needn't show every extreme that they name: Among the 32 blocks of one device no owner is named more than 2 times, a bound that some block reaches. `counts`: the first block of every device is full.
All inputs are finite; a program needn't handle non-finite values.
Results may differ from the reference program's by a relative error of at most 0.0017.
Values may be sent and summed in bfloat16 or wider, within the bound.
A program may use at most 256 MiB of HBM per device.

```python
import math
import jax
import jax.numpy as jnp
import numpy as np
from jax import lax

FIELDS = 4
LEV = 90
PCS = 300
LAT_DEV = 8
LON_DEV = 128
SND = 128
CAP = 2
STEPS = 4
NB_DEV = 32
NLAT = 32
NLON = 1024
BLOCKS = 1024
N_LON = 8
DEVICES = 32


def draw_counts(key, part):
    values = jax.random.randint(key, (BLOCKS,), 1, SND + 1, dtype=jnp.int32)
    return values.at[::NB_DEV].set(SND)


def place_ends(drawn, key, low, top_value):
    extent = drawn.shape
    index_at = [jax.random.randint(jax.random.fold_in(key, axis), (), 0, extent[axis]) for axis in range(len(extent))]
    drawn = drawn.at[tuple(index_at)].set(low)
    longest = extent.index(max(extent))
    index_at[longest] = (index_at[longest] + 1) % extent[longest]
    return drawn.at[tuple(index_at)].set(top_value)


def shard_levels(stream_key, shape, shards, smallest, largest):
    def one(dim, shards_of):
        heights = jax.random.uniform(jax.random.fold_in(jax.random.fold_in(stream_key, 6), dim), (shards_of,), jnp.float32, smallest / len(shards), largest / len(shards))
        return jnp.repeat(jnp.exp(heights), shape[dim] // shards_of).reshape((-1,) + (1,) * (len(shape) - dim - 1))

    level = one(*shards[0])
    for cut in shards[1:]:
        level = level * one(*cut)
    return level


def shared_out(stream_key, own, number, rows, amount, top, reach, skew):
    ranking = jax.random.permutation(stream_key, amount)
    packed, ordinary = load_shares(amount, rows * top, reach, skew, True), load_shares(amount, rows * top, reach, skew, False)
    places = jnp.arange(amount)

    def named(lengths, rotation):
        used = int((lengths > 0).sum())
        fixed = max(1, used // 4)
        passed = fixed + (places - fixed + rotation * (used - fixed)) % max(1, amount - fixed)
        return jnp.zeros((amount,), jnp.int32).at[ranking[jnp.where(places < fixed, places, passed)]].set(jnp.asarray(lengths, jnp.int32))

    lengths = jnp.where(number % 4 == 0, named(packed, number // 4), named(ordinary, number - number // 4 - 1))
    mixed = jax.random.permutation(jax.random.fold_in(own, 3), amount)
    source_of, taker = mixed[0:amount // 2 * 2:2], mixed[1:amount // 2 * 2:2]
    room = jnp.minimum(lengths[source_of] - 1, reach - lengths[taker]) // 2
    room = jnp.where((source_of == ranking[0]) | (taker == ranking[0]) | (lengths[taker] == 0), 0, jnp.maximum(room, 0))
    passed = jax.random.randint(jax.random.fold_in(own, 4), (amount // 2,), 0, 1 << 20) % (room + 1)
    lengths = lengths.at[source_of].add(-passed).at[taker].add(passed)
    items = jnp.searchsorted(jnp.cumsum(lengths), jnp.arange(rows * top), side="right").astype(jnp.int32)
    table = items.reshape(top, rows).T
    table = table[jax.random.permutation(jax.random.fold_in(own, 1), rows)]
    rotation = jax.random.randint(jax.random.fold_in(own, 2), (rows, 1), 0, top)
    return jnp.take_along_axis(table, (jnp.arange(top)[None, :] + rotation) % top, axis=1)


def load_shares(count, total, reach, slope, full):
    portions = [(1 << 20) // math.isqrt(rank ** slope) + 1 for rank in range(1, count + 1)]
    largest = reach if full else min(reach, max(-(-total // count), total * portions[0] // sum(portions)))
    least = 1 if total - largest >= count - 1 else 0
    holding, surplus = [largest] + [least] * (count - 1), total - largest - least * (count - 1)
    while surplus > 0:
        free = [i for i in range(1, count) if holding[i] < largest] or [i for i in range(1, count) if holding[i] < reach]
        mass, remaining = sum([portions[i] for i in free]), surplus
        for i in free:
            extra = min(reach - holding[i], max(1, remaining * portions[i] // mass), surplus)
            holding[i] = holding[i] + extra
            surplus = surplus - extra
    return np.array(holding)


def bell_draw(rng, extent, scale, limit, shards=(), held_as=jnp.bfloat16):
    entries = jax.random.normal(rng, extent, jnp.float32) * scale
    if len(shards) > 0:
        entries = shard_levels(rng, extent, shards, -0.22, 0.18) * entries
    return jnp.clip(entries, min=-limit, max=limit).astype(held_as)


def setup_inputs(seed: int = 0) -> dict:
    key_list = jax.random.split(jax.random.key(seed), 9)
    control = bell_draw(key_list[0], (FIELDS, LEV, NLAT, NLON), 1.0, 6.0, ((2, 4), (3, 8)), jnp.float32)
    kappa = jnp.clip(jnp.exp(math.log(0.5) - 0.6931472 * jax.random.uniform(key_list[1], (FIELDS, LEV, NLAT, NLON), jnp.float32) ** shard_levels(key_list[1], (FIELDS, LEV, NLAT, NLON), ((2, 4), (3, 8)), -0.2, 0.2)), 0.25, 0.5)
    pc_obs = bell_draw(key_list[2], (BLOCKS, SND, PCS), 1.0, 6.0, ((0, 32),))
    owner_keys = jax.random.split(jax.random.fold_in(key_list[3], 1), BLOCKS // NB_DEV)
    owner_turns = jax.random.permutation(jax.random.fold_in(key_list[3], 3), BLOCKS // NB_DEV)
    owner = jax.vmap(lambda own, number: shared_out(jax.random.fold_in(key_list[3], 2), own, number, NB_DEV, DEVICES, 1, CAP, 2))(owner_keys, owner_turns).reshape((BLOCKS, 1))
    columns = place_ends(jax.random.randint(key_list[4], (BLOCKS, SND), 0, LAT_DEV * LON_DEV), jax.random.fold_in(key_list[4], 1), 0, (LAT_DEV * LON_DEV) - 1).astype(jnp.int32)
    counts = draw_counts(jax.random.fold_in(key_list[8], 71), 0)
    jacobian = bell_draw(key_list[6], (FIELDS * LEV, PCS), (FIELDS * LEV) ** -0.5, 0.3125)
    obs_weight = jnp.clip(jnp.exp(jax.random.uniform(key_list[7], (PCS,), jnp.float32, math.log(0.3), math.log(3.0))), 0.3, 3.0)
    return dict(control=control, kappa=kappa, pc_obs=pc_obs, owner=owner, columns=columns, counts=counts, jacobian=jacobian, obs_weight=obs_weight)


def relax(field, coef):
    centre = field[..., 1:-1, 1:-1]
    inner = coef[..., 1:-1, 1:-1]
    result = centre + inner * coef[..., :-2, 1:-1] * (field[..., :-2, 1:-1] - centre)
    result = result + inner * coef[..., 2:, 1:-1] * (field[..., 2:, 1:-1] - centre)
    result = result + inner * coef[..., 1:-1, :-2] * (field[..., 1:-1, :-2] - centre)
    result = result + inner * coef[..., 1:-1, 2:] * (field[..., 1:-1, 2:] - centre)
    return result


def pad_grid(plane):
    plane = jnp.pad(plane, ((1, 1), (0, 0)))
    return jnp.concatenate([plane[:, -1:], plane, plane[:, :1]], axis=1)


def spread(pair):
    field, coef = pair
    coef_pad = pad_grid(coef)
    for repeat in range(STEPS):
        field = relax(pad_grid(field), coef_pad)
    return field


def reference(control, kappa, pc_obs, owner, columns, counts, jacobian, obs_weight):
    depth = FIELDS * LEV
    flat_v = control.reshape(depth, NLAT, NLON)
    flat_k = kappa.reshape(depth, NLAT, NLON)
    state = lax.map(spread, (flat_v, flat_k))
    state_b = state.astype(jnp.bfloat16).reshape(depth, NLAT * NLON)
    order = jnp.arange(SND, dtype=jnp.int32)

    def visit(total, item):
        own, cols, count_part, obs_part = item
        glat = ((own // N_LON) * LAT_DEV)[:, None] + cols // LON_DEV
        glon = ((own % N_LON) * LON_DEV)[:, None] + cols % LON_DEV
        cell = (glat * NLON + glon).reshape(-1).astype(jnp.int32)
        picked = state_b[:, cell]
        model = lax.dot_general(picked, jacobian, (((0,), (0,)), ((), ())), preferred_element_type=jnp.float32)
        valid = (order[None, :] < count_part[:, None]).astype(jnp.float32).reshape(-1, 1)
        misfit = (model - obs_part.reshape(-1, PCS).astype(jnp.float32)) * obs_weight[None, :] * valid
        return total.at[cell].add(misfit), None

    start = jnp.zeros((NLAT * NLON, PCS), jnp.float32)
    items = (owner[:, 0].reshape(DEVICES, NB_DEV), columns.reshape(DEVICES, NB_DEV, SND),
             counts.reshape(DEVICES, NB_DEV), pc_obs.reshape(DEVICES, NB_DEV, SND, PCS))
    total = lax.scan(visit, start, items)[0]
    back = lax.dot_general(jacobian, total.astype(jnp.bfloat16), (((1,), (1,)), ((), ())),
                           preferred_element_type=jnp.float32)
    adjoint = lax.map(spread, (back.reshape(depth, NLAT, NLON), flat_k))
    return control + adjoint.reshape(control.shape)
```

```python
import jax
import jax.numpy as jnp
from jax import lax
from jax.experimental import pallas as pl
from jax.experimental.pallas import tpu as pltpu
from jax.sharding import PartitionSpec as P

CAP = 2
STEPS = 4
GROUP = 4


def extended(cells, sides, width):
    for axis, dim in sides:
        count = lax.axis_size(axis)
        head = lax.slice_in_dim(cells, 0, width, axis=dim)
        tail = lax.slice_in_dim(cells, cells.shape[dim] - width, cells.shape[dim], axis=dim)
        cells = jnp.concatenate(
            [
                lax.ppermute(tail, axis, [(i, (i + 1) % count) for i in range(count)]),
                cells,
                lax.ppermute(head, axis, [((i + 1) % count, i) for i in range(count)]),
            ],
            axis=dim,
        )
    return cells


def weights_of(coef):
    inner = coef[..., 1:-1, 1:-1]
    return (
        inner * coef[..., :-2, 1:-1],
        inner * coef[..., 2:, 1:-1],
        inner * coef[..., 1:-1, :-2],
        inner * coef[..., 1:-1, 2:],
    )


def relax(field, weights):
    north, south, west, east = weights
    centre = field[..., 1:-1, 1:-1]
    result = centre + north * (field[..., :-2, 1:-1] - centre)
    result = result + south * (field[..., 2:, 1:-1] - centre)
    result = result + west * (field[..., 1:-1, :-2] - centre)
    result = result + east * (field[..., 1:-1, 2:] - centre)
    return result


def spread(field, coef):
    for repeat in range(STEPS):
        inset = slice(repeat, coef.shape[-2] - repeat), slice(repeat, coef.shape[-1] - repeat)
        field = relax(field, weights_of(coef[..., inset[0], inset[1]]))
    return field


def close_rims(coef, width):
    extent = coef.shape[2]
    lat_pos = lax.axis_index("lat")
    line = lax.broadcasted_iota(jnp.int32, (extent, 1), 0)
    outside = (line < width) & (lat_pos == 0) | (line >= extent - width) & (
        lat_pos == lax.axis_size("lat") - 1
    )
    return jnp.where(outside, jnp.float32(0.0), coef)


def pack_kernel(source_ref, *refs):
    blocks, (code_ref, out_ref, wide) = refs[:CAP], refs[CAP:]
    comps = blocks[0].shape[2]
    for k, block in enumerate(blocks):
        wide[0:comps, :] = jnp.transpose(block[0].astype(jnp.float32))
        code = code_ref[0, k : k + 1, :]
        low = jnp.bitwise_and(code, 31)
        wide[comps : comps + 1, :] = jnp.ones((1, wide.shape[1]), jnp.float32)
        wide[comps + 1 : comps + 2, :] = jnp.right_shift(code - low, 5).astype(jnp.float32)
        wide[comps + 2 : comps + 3, :] = low.astype(jnp.float32)
        wide[comps + 3 :, :] = jnp.zeros((wide.shape[0] - comps - 3, wide.shape[1]), jnp.float32)
        out_ref[k] = wide[...].astype(jnp.bfloat16)


def pack(pc_obs, source, code, height):
    blocks, soundings, comps = pc_obs.shape
    slots = code.shape[0]

    def place(k):
        return lambda i, src: (src[i * CAP + k], 0, 0)

    return pl.pallas_call(
        pack_kernel,
        out_shape=jax.ShapeDtypeStruct((slots, height, soundings), jnp.bfloat16),
        grid_spec=pltpu.PrefetchScalarGridSpec(
            num_scalar_prefetch=1,
            grid=(slots // CAP,),
            in_specs=[pl.BlockSpec((1, soundings, comps), place(k)) for k in range(CAP)]
            + [pl.BlockSpec((1, CAP, soundings), lambda i, src: (i, 0, 0))],
            out_specs=pl.BlockSpec((CAP, height, soundings), lambda i, src: (i, 0, 0)),
            scratch_shapes=[pltpu.VMEM((height, soundings), jnp.float32)],
        ),
    )(source, *([pc_obs] * CAP), code.reshape(slots // CAP, CAP, soundings))


def gather_kernel(comps, got_ref, sums_ref):
    height, cells = sums_ref.shape

    @pl.when(pl.program_id(0) == 0)
    def _():
        sums_ref[...] = jnp.zeros_like(sums_ref)

    base = height - 16
    lines = []
    for k in range(GROUP):
        tail = got_ref[k, base:height, :].astype(jnp.float32)
        high = tail[comps + 1 - base : comps + 2 - base, :]
        lines.append((high * 32.0 + tail[comps + 2 - base : comps + 3 - base, :]).astype(jnp.int32))
    code = jnp.concatenate(lines, axis=1)
    cell = lax.broadcasted_iota(jnp.int32, (cells, code.shape[1]), 0)
    hot = jnp.where(cell == code, 1.0, 0.0).astype(jnp.bfloat16)
    obs = jnp.concatenate([got_ref[k] for k in range(GROUP)], axis=1)
    sums_ref[...] += lax.dot_general(
        obs, hot, (((1,), (1,)), ((), ())), preferred_element_type=jnp.float32
    )


def column_sums(got, comps, cells):
    slots, height, soundings = got.shape
    return pl.pallas_call(
        lambda *refs: gather_kernel(comps, *refs),
        out_shape=jax.ShapeDtypeStruct((height, cells), jnp.float32),
        grid=(slots // GROUP,),
        in_specs=[pl.BlockSpec((GROUP, height, soundings), lambda i: (i, 0, 0))],
        out_specs=pl.BlockSpec((height, cells), lambda i: (0, 0)),
        compiler_params=pltpu.CompilerParams(vmem_limit_bytes=32 * 2**20),
    )(got)


def per_device(control, kappa, pc_obs, owner, columns, counts, jacobian, obs_weight):
    peers = lax.axis_size("lat") * lax.axis_size("lon")
    fields, levels, rows, width_dev = control.shape
    blocks, soundings, comps = pc_obs.shape
    cells = rows * width_dev
    height = -(-(comps + 3) // 16) * 16
    slots = peers * CAP
    target = owner[:, 0]
    index = jnp.arange(blocks, dtype=jnp.int32)
    same = (target[:, None] == target[None, :]) & (index[None, :] < index[:, None])
    position = target * CAP + jnp.sum(same.astype(jnp.int32), axis=1)
    hits = position[None, :] == jnp.arange(slots, dtype=jnp.int32)[:, None]
    source = jnp.sum(jnp.where(hits, index[None, :], 0), axis=1)
    order = jnp.arange(soundings, dtype=jnp.int32)
    code = jnp.where(order[None, :] < counts[:, None], columns, -32)
    code = -32 + jnp.sum(jnp.where(hits[:, :, None], code[None] + 32, 0), axis=1)
    sent = pack(pc_obs, source, code, height)
    got = lax.all_to_all(sent, ("lat", "lon"), split_axis=0, concat_axis=0, tiled=True)

    sides = (("lat", 2), ("lon", 3))
    padded = extended(jnp.concatenate([control, kappa], axis=0), sides, STEPS)
    coef = close_rims(padded[fields:], STEPS)
    state = spread(padded[:fields], coef)
    table = state.astype(jnp.bfloat16).reshape(fields * levels, cells)
    model = lax.dot_general(
        jacobian, table, (((0,), (0,)), ((), ())), preferred_element_type=jnp.float32
    )
    sums = column_sums(got, comps, cells)
    total = (sums[comps : comps + 1] * model - sums[:comps]) * obs_weight[:, None]
    total = total.astype(jnp.bfloat16).reshape(1, comps, rows, width_dev)
    total = extended(total, sides, STEPS)
    back = lax.dot_general(
        jacobian, total[0], (((1,), (0,)), ((), ())), preferred_element_type=jnp.float32
    )
    adjoint = spread(back.reshape((fields, levels) + back.shape[1:]), coef)
    return control + adjoint


def solution(mesh):
    placed = (
        P(None, None, "lat", "lon"),
        P(None, None, "lat", "lon"),
        P(("lat", "lon"), None, None),
        P(("lat", "lon"), None),
        P(("lat", "lon"), None),
        P(("lat", "lon")),
        P(),
        P(),
    )
    return jax.shard_map(
        per_device,
        mesh=mesh,
        in_specs=placed,
        out_specs=P(None, None, "lat", "lon"),
        check_vma=False,
    )
```

```python
import jax
import jax.numpy as jnp
from jax import lax
from jax.experimental import pallas as pl
from jax.experimental.pallas import tpu as pltpu
from jax.sharding import PartitionSpec as P

CAP = 2
STEPS = 4
GROUP = 4


def ring(axis, step):
    count = lax.axis_size(axis)
    return [(i, (i + step) % count) for i in range(count)]


def rims(core, closed):
    north = lax.ppermute(core[:, -STEPS:], "lat", ring("lat", 1))
    south = lax.ppermute(core[:, :STEPS], "lat", ring("lat", -1))
    if closed:
        place = lax.axis_index("lat")
        zero = jnp.zeros((), core.dtype)
        north = jnp.where(place == 0, zero, north)
        south = jnp.where(place == lax.axis_size("lat") - 1, zero, south)
    main = jnp.concatenate([core, south, north], axis=1)
    planes = main.shape[0]
    head = main[:, :, :STEPS].reshape(planes, -1)
    tail = main[:, :, -STEPS:].reshape(planes, -1)
    west = lax.ppermute(tail, "lon", ring("lon", 1))
    east = lax.ppermute(head, "lon", ring("lon", -1))
    return main, jnp.concatenate([east, west], axis=1)


def side_tile(side, rows, width):
    planes = side.shape[0]
    parts = side.reshape(planes, 2, rows, STEPS)
    gap = jnp.zeros((planes, rows, width - 2 * STEPS), side.dtype)
    return jnp.concatenate([parts[:, 0], gap, parts[:, 1]], axis=2)


def spread_kernel(field_ref, side_ref, coef_ref, coef_side_ref, *refs):
    out_ref = refs[-1]
    core, width = out_ref.shape[1:]
    rows, lanes = field_ref.shape[1], 2 * width

    @pl.loop(0, out_ref.shape[0], unroll=4)
    def _(i):
        coef = jnp.concatenate([coef_ref[i], coef_side_ref[i]], axis=1)
        field = jnp.concatenate([field_ref[i], side_ref[i]], axis=1)
        south = coef * pltpu.roll(coef, rows - 1, 0)
        east = coef * pltpu.roll(coef, lanes - 1, 1)
        for repeat in range(STEPS):
            down = south * (pltpu.roll(field, rows - 1, 0) - field)
            along = east * (pltpu.roll(field, lanes - 1, 1) - field)
            field = field + (down - pltpu.roll(down, 1, 0)) + (along - pltpu.roll(along, 1, 1))
        result = field[:core, :width]
        out_ref[i] = result + refs[0][i] if len(refs) > 1 else result


def spread(field, side, coef, coef_side, core, *base):
    planes, rows, width = field.shape
    batch = max(n for n in range(4, 41, 4) if planes % n == 0)
    wide = pl.BlockSpec((batch, rows, width), lambda i: (i, 0, 0))
    thin = pl.BlockSpec((batch, core, width), lambda i: (i, 0, 0))
    return pl.pallas_call(
        spread_kernel,
        out_shape=jax.ShapeDtypeStruct((planes, core, width), jnp.float32),
        grid=(planes // batch,),
        in_specs=[wide] * 4 + [thin] * len(base),
        out_specs=thin,
        cost_estimate=pl.CostEstimate(
            flops=planes * rows * width * 80, bytes_accessed=planes * rows * width * 20, transcendentals=0
        ),
    )(field, side, coef, coef_side, *base)


def pack_kernel(source_ref, *refs):
    blocks, (code_ref, out_ref, wide) = refs[:CAP], refs[CAP:]
    comps = blocks[0].shape[2]
    for k, block in enumerate(blocks):
        wide[0:comps, :] = jnp.transpose(block[0].astype(jnp.float32))
        code = code_ref[0, k : k + 1, :]
        low = jnp.bitwise_and(code, 31)
        wide[comps : comps + 1, :] = jnp.ones((1, wide.shape[1]), jnp.float32)
        wide[comps + 1 : comps + 2, :] = jnp.right_shift(code - low, 5).astype(jnp.float32)
        wide[comps + 2 : comps + 3, :] = low.astype(jnp.float32)
        wide[comps + 3 :, :] = jnp.zeros((wide.shape[0] - comps - 3, wide.shape[1]), jnp.float32)
        out_ref[k] = wide[...].astype(jnp.bfloat16)


def pack(pc_obs, source, code, height):
    blocks, soundings, comps = pc_obs.shape
    slots = code.shape[0]

    def place(k):
        return lambda i, src: (src[i * CAP + k], 0, 0)

    return pl.pallas_call(
        pack_kernel,
        out_shape=jax.ShapeDtypeStruct((slots, height, soundings), jnp.bfloat16),
        grid_spec=pltpu.PrefetchScalarGridSpec(
            num_scalar_prefetch=1,
            grid=(slots // CAP,),
            in_specs=[pl.BlockSpec((1, soundings, comps), place(k)) for k in range(CAP)]
            + [pl.BlockSpec((1, CAP, soundings), lambda i, src: (i, 0, 0))],
            out_specs=pl.BlockSpec((CAP, height, soundings), lambda i, src: (i, 0, 0)),
            scratch_shapes=[pltpu.VMEM((height, soundings), jnp.float32)],
        ),
    )(source, *([pc_obs] * CAP), code.reshape(slots // CAP, CAP, soundings))


def gather_kernel(comps, got_ref, sums_ref):
    height, cells = sums_ref.shape

    @pl.when(pl.program_id(0) == 0)
    def _():
        sums_ref[...] = jnp.zeros_like(sums_ref)

    base = height - 16
    lines = []
    for k in range(GROUP):
        tail = got_ref[k, base:height, :].astype(jnp.float32)
        high = tail[comps + 1 - base : comps + 2 - base, :]
        lines.append((high * 32.0 + tail[comps + 2 - base : comps + 3 - base, :]).astype(jnp.int32))
    code = jnp.concatenate(lines, axis=1)
    cell = lax.broadcasted_iota(jnp.int32, (cells, code.shape[1]), 0)
    hot = jnp.where(cell == code, 1.0, 0.0).astype(jnp.bfloat16)
    obs = jnp.concatenate([got_ref[k] for k in range(GROUP)], axis=1)
    sums_ref[...] += lax.dot_general(
        obs, hot, (((1,), (1,)), ((), ())), preferred_element_type=jnp.float32
    )


def column_sums(got, comps, cells):
    slots, height, soundings = got.shape
    return pl.pallas_call(
        lambda *refs: gather_kernel(comps, *refs),
        out_shape=jax.ShapeDtypeStruct((height, cells), jnp.float32),
        grid=(slots // GROUP,),
        in_specs=[pl.BlockSpec((GROUP, height, soundings), lambda i: (i, 0, 0))],
        out_specs=pl.BlockSpec((height, cells), lambda i: (0, 0)),
        compiler_params=pltpu.CompilerParams(vmem_limit_bytes=32 * 2**20),
    )(got)


def per_device(control, kappa, pc_obs, owner, columns, counts, jacobian, obs_weight):
    peers = lax.axis_size("lat") * lax.axis_size("lon")
    fields, levels, rows, width_dev = control.shape
    blocks, soundings, comps = pc_obs.shape
    cells = rows * width_dev
    height = -(-(comps + 3) // 16) * 16
    slots = peers * CAP
    target = owner[:, 0]
    index = jnp.arange(blocks, dtype=jnp.int32)
    same = (target[:, None] == target[None, :]) & (index[None, :] < index[:, None])
    position = target * CAP + jnp.sum(same.astype(jnp.int32), axis=1)
    hits = position[None, :] == jnp.arange(slots, dtype=jnp.int32)[:, None]
    source = jnp.sum(jnp.where(hits, index[None, :], 0), axis=1)
    order = jnp.arange(soundings, dtype=jnp.int32)
    code = jnp.where(order[None, :] < counts[:, None], columns, -32)
    code = -32 + jnp.sum(jnp.where(hits[:, :, None], code[None] + 32, 0), axis=1)
    sent = pack(pc_obs, source, code, height)
    got = lax.all_to_all(sent, ("lat", "lon"), split_axis=0, concat_axis=0, tiled=True)

    planes = fields * levels
    extent = rows + 2 * STEPS
    start = control.reshape(planes, rows, width_dev)
    field, side = rims(start, False)
    coef, coef_side = rims(kappa.reshape(planes, rows, width_dev), True)
    coef_side = side_tile(coef_side, extent, width_dev)
    state = spread(field, side_tile(side, extent, width_dev), coef, coef_side, rows)
    table = state.astype(jnp.bfloat16).reshape(planes, cells)
    model = lax.dot_general(
        jacobian, table, (((0,), (0,)), ((), ())), preferred_element_type=jnp.float32
    )
    sums = column_sums(got, comps, cells)
    total = (sums[comps : comps + 1] * model - sums[:comps]) * obs_weight[:, None]
    total = total.astype(jnp.bfloat16).reshape(comps, rows, width_dev)
    total, total_side = rims(total, False)
    back, back_side = (
        lax.dot_general(
            jacobian, part.reshape(comps, -1), (((1,), (0,)), ((), ())), preferred_element_type=jnp.float32
        )
        for part in (total, total_side)
    )
    back = back.reshape(planes, extent, width_dev)
    result = spread(back, side_tile(back_side, extent, width_dev), coef, coef_side, rows, start)
    return result.reshape(control.shape)


def solution(mesh):
    placed = (
        P(None, None, "lat", "lon"),
        P(None, None, "lat", "lon"),
        P(("lat", "lon"), None, None),
        P(("lat", "lon"), None),
        P(("lat", "lon"), None),
        P(("lat", "lon")),
        P(),
        P(),
    )
    return jax.shard_map(
        per_device,
        mesh=mesh,
        in_specs=placed,
        out_specs=P(None, None, "lat", "lon"),
        check_vma=False,
    )
```

```python
import jax
import jax.numpy as jnp
from jax import lax
from jax.experimental import pallas as pl
from jax.experimental.pallas import tpu as pltpu
from jax.sharding import PartitionSpec as P

CAP = 2
STEPS = 4
GROUP = 4


def ring(axis, step):
    count = lax.axis_size(axis)
    return [(i, (i + step) % count) for i in range(count)]


def rims(core, closed):
    north = lax.ppermute(core[:, -STEPS:], "lat", ring("lat", 1))
    south = lax.ppermute(core[:, :STEPS], "lat", ring("lat", -1))
    if closed:
        place = lax.axis_index("lat")
        zero = jnp.zeros((), core.dtype)
        north = jnp.where(place == 0, zero, north)
        south = jnp.where(place == lax.axis_size("lat") - 1, zero, south)
    main = jnp.concatenate([core, south, north], axis=1)
    planes = main.shape[0]
    head = main[:, :, :STEPS].reshape(planes, -1)
    tail = main[:, :, -STEPS:].reshape(planes, -1)
    west = lax.ppermute(tail, "lon", ring("lon", 1))
    east = lax.ppermute(head, "lon", ring("lon", -1))
    return main, jnp.concatenate([east, west], axis=1)


def side_tile(side, rows, width):
    planes = side.shape[0]
    parts = side.reshape(planes, 2, rows, STEPS)
    gap = jnp.zeros((planes, rows, width - 2 * STEPS), side.dtype)
    return jnp.concatenate([parts[:, 0], gap, parts[:, 1]], axis=2)


def spread_kernel(field_ref, side_ref, coef_ref, coef_side_ref, *refs):
    out_ref = refs[-1]
    core, width = out_ref.shape[1:]
    rows, lanes = field_ref.shape[1], 2 * width

    @pl.loop(0, out_ref.shape[0], unroll=4)
    def _(i):
        coef = jnp.concatenate([coef_ref[i], coef_side_ref[i]], axis=1)
        field = jnp.concatenate([field_ref[i], side_ref[i]], axis=1)
        south = coef * pltpu.roll(coef, rows - 1, 0)
        east = coef * pltpu.roll(coef, lanes - 1, 1)
        for repeat in range(STEPS):
            down = south * (pltpu.roll(field, rows - 1, 0) - field)
            along = east * (pltpu.roll(field, lanes - 1, 1) - field)
            field = field + (down - pltpu.roll(down, 1, 0)) + (along - pltpu.roll(along, 1, 1))
        result = field[:core, :width]
        out_ref[i] = result + refs[0][i] if len(refs) > 1 else result


def spread(field, side, coef, coef_side, core, *base):
    planes, rows, width = field.shape
    batch = max(n for n in range(4, 41, 4) if planes % n == 0)
    wide = pl.BlockSpec((batch, rows, width), lambda i: (i, 0, 0))
    thin = pl.BlockSpec((batch, core, width), lambda i: (i, 0, 0))
    return pl.pallas_call(
        spread_kernel,
        out_shape=jax.ShapeDtypeStruct((planes, core, width), jnp.float32),
        grid=(planes // batch,),
        in_specs=[wide] * 4 + [thin] * len(base),
        out_specs=thin,
        cost_estimate=pl.CostEstimate(
            flops=planes * rows * width * 80, bytes_accessed=planes * rows * width * 20, transcendentals=0
        ),
    )(field, side, coef, coef_side, *base)


def pack_kernel(source_ref, *refs):
    blocks, (code_ref, out_ref, wide) = refs[:CAP], refs[CAP:]
    comps = blocks[0].shape[2]
    for k, block in enumerate(blocks):
        wide[0:comps, :] = jnp.transpose(block[0].astype(jnp.float32))
        code = code_ref[0, k : k + 1, :]
        low = jnp.bitwise_and(code, 31)
        wide[comps : comps + 1, :] = jnp.ones((1, wide.shape[1]), jnp.float32)
        wide[comps + 1 : comps + 2, :] = jnp.right_shift(code - low, 5).astype(jnp.float32)
        wide[comps + 2 : comps + 3, :] = low.astype(jnp.float32)
        wide[comps + 3 :, :] = jnp.zeros((wide.shape[0] - comps - 3, wide.shape[1]), jnp.float32)
        out_ref[k] = wide[...].astype(jnp.bfloat16)


def pack(pc_obs, source, code, height):
    blocks, soundings, comps = pc_obs.shape
    slots = code.shape[0]

    def place(k):
        return lambda i, src: (src[i * CAP + k], 0, 0)

    return pl.pallas_call(
        pack_kernel,
        out_shape=jax.ShapeDtypeStruct((slots, height, soundings), jnp.bfloat16),
        grid_spec=pltpu.PrefetchScalarGridSpec(
            num_scalar_prefetch=1,
            grid=(slots // CAP,),
            in_specs=[pl.BlockSpec((1, soundings, comps), place(k)) for k in range(CAP)]
            + [pl.BlockSpec((1, CAP, soundings), lambda i, src: (i, 0, 0))],
            out_specs=pl.BlockSpec((CAP, height, soundings), lambda i, src: (i, 0, 0)),
            scratch_shapes=[pltpu.VMEM((height, soundings), jnp.float32)],
        ),
    )(source, *([pc_obs] * CAP), code.reshape(slots // CAP, CAP, soundings))


def gather_kernel(comps, got_ref, sums_ref):
    height, cells = sums_ref.shape

    @pl.when(pl.program_id(0) == 0)
    def _():
        sums_ref[...] = jnp.zeros_like(sums_ref)

    base = height - 16
    lines = []
    for k in range(GROUP):
        tail = got_ref[k, base:height, :].astype(jnp.float32)
        high = tail[comps + 1 - base : comps + 2 - base, :]
        lines.append((high * 32.0 + tail[comps + 2 - base : comps + 3 - base, :]).astype(jnp.int32))
    code = jnp.concatenate(lines, axis=1)
    cell = lax.broadcasted_iota(jnp.int32, (cells, code.shape[1]), 0)
    hot = jnp.where(cell == code, 1.0, 0.0).astype(jnp.bfloat16)
    obs = jnp.concatenate([got_ref[k] for k in range(GROUP)], axis=1)
    sums_ref[...] += lax.dot_general(
        obs, hot, (((1,), (1,)), ((), ())), preferred_element_type=jnp.float32
    )


def column_sums(got, comps, cells):
    slots, height, soundings = got.shape
    return pl.pallas_call(
        lambda *refs: gather_kernel(comps, *refs),
        out_shape=jax.ShapeDtypeStruct((height, cells), jnp.float32),
        grid=(slots // GROUP,),
        in_specs=[pl.BlockSpec((GROUP, height, soundings), lambda i: (i, 0, 0))],
        out_specs=pl.BlockSpec((height, cells), lambda i: (0, 0)),
        compiler_params=pltpu.CompilerParams(vmem_limit_bytes=32 * 2**20),
    )(got)


def per_device(control, kappa, pc_obs, owner, columns, counts, jacobian, obs_weight):
    peers = lax.axis_size("lat") * lax.axis_size("lon")
    fields, levels, rows, width_dev = control.shape
    blocks, soundings, comps = pc_obs.shape
    cells = rows * width_dev
    height = -(-(comps + 3) // 16) * 16
    slots = peers * CAP
    target = owner[:, 0]
    index = jnp.arange(blocks, dtype=jnp.int32)
    same = (target[:, None] == target[None, :]) & (index[None, :] < index[:, None])
    position = target * CAP + jnp.sum(same.astype(jnp.int32), axis=1)
    hits = position[None, :] == jnp.arange(slots, dtype=jnp.int32)[:, None]
    source = jnp.sum(jnp.where(hits, index[None, :], 0), axis=1)
    order = jnp.arange(soundings, dtype=jnp.int32)
    code = jnp.where(order[None, :] < counts[:, None], columns, -32)
    code = -32 + jnp.sum(jnp.where(hits[:, :, None], code[None] + 32, 0), axis=1)
    sent = pack(pc_obs, source, code, height)
    planes = fields * levels
    extent = rows + 2 * STEPS
    start = control.reshape(planes, rows, width_dev)
    field, side = rims(start, False)
    coef, coef_side = rims(kappa.reshape(planes, rows, width_dev), True)
    sent, side, coef_side = lax.optimization_barrier((sent, side, coef_side))
    got = lax.all_to_all(sent, ("lat", "lon"), split_axis=0, concat_axis=0, tiled=True)
    coef_side = side_tile(coef_side, extent, width_dev)
    state = spread(field, side_tile(side, extent, width_dev), coef, coef_side, rows)
    table = state.astype(jnp.bfloat16).reshape(planes, cells)
    model = lax.dot_general(
        jacobian, table, (((0,), (0,)), ((), ())), preferred_element_type=jnp.float32
    )
    sums = column_sums(got, comps, cells)
    total = (sums[comps : comps + 1] * model - sums[:comps]) * obs_weight[:, None]
    total = total.astype(jnp.bfloat16).reshape(comps, rows, width_dev)
    total, total_side = rims(total, False)
    back, back_side = (
        lax.dot_general(
            jacobian, part.reshape(comps, -1), (((1,), (0,)), ((), ())), preferred_element_type=jnp.float32
        )
        for part in (total, total_side)
    )
    back = back.reshape(planes, extent, width_dev)
    result = spread(back, side_tile(back_side, extent, width_dev), coef, coef_side, rows, start)
    return result.reshape(control.shape)


def solution(mesh):
    placed = (
        P(None, None, "lat", "lon"),
        P(None, None, "lat", "lon"),
        P(("lat", "lon"), None, None),
        P(("lat", "lon"), None),
        P(("lat", "lon"), None),
        P(("lat", "lon")),
        P(),
        P(),
    )
    return jax.shard_map(
        per_device,
        mesh=mesh,
        in_specs=placed,
        out_specs=P(None, None, "lat", "lon"),
        check_vma=False,
    )
```

```python
import jax
import jax.numpy as jnp
from jax import lax
from jax.experimental import pallas as pl
from jax.experimental.pallas import tpu as pltpu
from jax.sharding import PartitionSpec as P

CAP = 2
STEPS = 4
GROUP = 4


def ring(axis, step):
    count = lax.axis_size(axis)
    return [(i, (i + step) % count) for i in range(count)]


def rims(core, closed):
    north = lax.ppermute(core[:, -STEPS:], "lat", ring("lat", 1))
    south = lax.ppermute(core[:, :STEPS], "lat", ring("lat", -1))
    if closed:
        place = lax.axis_index("lat")
        zero = jnp.zeros((), core.dtype)
        north = jnp.where(place == 0, zero, north)
        south = jnp.where(place == lax.axis_size("lat") - 1, zero, south)
    main = jnp.concatenate([core, south, north], axis=1)
    planes = main.shape[0]
    head = main[:, :, :STEPS].reshape(planes, -1)
    tail = main[:, :, -STEPS:].reshape(planes, -1)
    west = lax.ppermute(tail, "lon", ring("lon", 1))
    east = lax.ppermute(head, "lon", ring("lon", -1))
    return main, jnp.concatenate([east, west], axis=1)


def strips(main, side, fields):
    planes, rows, width = main.shape
    levels, near = planes // fields, 3 * STEPS
    body = main.reshape(fields, levels, rows, width)
    flat = side.reshape(fields, levels, 2, rows, STEPS)
    pieces = []
    for f in range(fields):
        pieces += [flat[f, :, 1], body[f, :, :, :near], body[f, :, :, width - near :], flat[f, :, 0]]
    return jnp.concatenate(pieces, axis=2)


def diffused(field, coef):
    rows, lanes = field.shape
    south = coef * pltpu.roll(coef, rows - 1, 0)
    east = coef * pltpu.roll(coef, lanes - 1, 1)
    for repeat in range(STEPS):
        down = south * (pltpu.roll(field, rows - 1, 0) - field)
        along = east * (pltpu.roll(field, lanes - 1, 1) - field)
        field = field + (down - pltpu.roll(down, 1, 0)) + (along - pltpu.roll(along, 1, 1))
    return field


def spread_kernel(field_ref, strip_ref, coef_ref, coef_strip_ref, *refs):
    out_ref = refs[-1]
    fields, levels, core, width = out_ref.shape
    slot = 8 * STEPS
    lane = lax.broadcasted_iota(jnp.int32, (core, width), 1)

    @pl.loop(0, levels)
    def _(i):
        edge = diffused(strip_ref[i], coef_strip_ref[i])[:core]
        for f in range(fields):
            result = diffused(field_ref[f, i], coef_ref[f, i])[:core]
            west = pltpu.roll(edge, (width - slot * f - STEPS) % width, 1)
            east = pltpu.roll(edge, (width - slot * f - slot + STEPS) % width, 1)
            result = jnp.where(lane < STEPS, west, result)
            result = jnp.where(lane >= width - STEPS, east, result)
            out_ref[f, i] = result + refs[0][f, i] if len(refs) > 1 else result


def spread(field, strip, coef, coef_strip, core, *base):
    planes, rows, width = field.shape
    levels = strip.shape[0]
    fields = planes // levels
    batch = max(n for n in range(1, 11) if levels % n == 0)
    wide = pl.BlockSpec((fields, batch, rows, width), lambda i: (0, i, 0, 0))
    edge = pl.BlockSpec((batch, rows, strip.shape[2]), lambda i: (i, 0, 0))
    thin = pl.BlockSpec((fields, batch, core, width), lambda i: (0, i, 0, 0))
    shape = (fields, levels, rows, width)
    return pl.pallas_call(
        spread_kernel,
        out_shape=jax.ShapeDtypeStruct((fields, levels, core, width), jnp.float32),
        grid=(levels // batch,),
        in_specs=[wide, edge, wide, edge] + [thin] * len(base),
        out_specs=thin,
        cost_estimate=pl.CostEstimate(
            flops=planes * rows * width * 50, bytes_accessed=planes * rows * width * 14, transcendentals=0
        ),
    )(field.reshape(shape), strip, coef.reshape(shape), coef_strip, *base)


def pack_kernel(source_ref, *refs):
    blocks, (code_ref, out_ref, wide) = refs[:CAP], refs[CAP:]
    comps = blocks[0].shape[2]
    for k, block in enumerate(blocks):
        wide[0:comps, :] = jnp.transpose(block[0].astype(jnp.float32))
        code = code_ref[0, k : k + 1, :]
        low = jnp.bitwise_and(code, 31)
        wide[comps : comps + 1, :] = jnp.ones((1, wide.shape[1]), jnp.float32)
        wide[comps + 1 : comps + 2, :] = jnp.right_shift(code - low, 5).astype(jnp.float32)
        wide[comps + 2 : comps + 3, :] = low.astype(jnp.float32)
        wide[comps + 3 :, :] = jnp.zeros((wide.shape[0] - comps - 3, wide.shape[1]), jnp.float32)
        out_ref[k] = wide[...].astype(jnp.bfloat16)


def pack(pc_obs, source, code, height):
    blocks, soundings, comps = pc_obs.shape
    slots = code.shape[0]

    def place(k):
        return lambda i, src: (src[i * CAP + k], 0, 0)

    return pl.pallas_call(
        pack_kernel,
        out_shape=jax.ShapeDtypeStruct((slots, height, soundings), jnp.bfloat16),
        grid_spec=pltpu.PrefetchScalarGridSpec(
            num_scalar_prefetch=1,
            grid=(slots // CAP,),
            in_specs=[pl.BlockSpec((1, soundings, comps), place(k)) for k in range(CAP)]
            + [pl.BlockSpec((1, CAP, soundings), lambda i, src: (i, 0, 0))],
            out_specs=pl.BlockSpec((CAP, height, soundings), lambda i, src: (i, 0, 0)),
            scratch_shapes=[pltpu.VMEM((height, soundings), jnp.float32)],
        ),
    )(source, *([pc_obs] * CAP), code.reshape(slots // CAP, CAP, soundings))


def gather_kernel(comps, got_ref, sums_ref):
    height, cells = sums_ref.shape

    @pl.when(pl.program_id(0) == 0)
    def _():
        sums_ref[...] = jnp.zeros_like(sums_ref)

    base = height - 16
    lines = []
    for k in range(GROUP):
        tail = got_ref[k, base:height, :].astype(jnp.float32)
        high = tail[comps + 1 - base : comps + 2 - base, :]
        lines.append((high * 32.0 + tail[comps + 2 - base : comps + 3 - base, :]).astype(jnp.int32))
    code = jnp.concatenate(lines, axis=1)
    cell = lax.broadcasted_iota(jnp.int32, (cells, code.shape[1]), 0)
    hot = jnp.where(cell == code, 1.0, 0.0).astype(jnp.bfloat16)
    obs = jnp.concatenate([got_ref[k] for k in range(GROUP)], axis=1)
    sums_ref[...] += lax.dot_general(
        obs, hot, (((1,), (1,)), ((), ())), preferred_element_type=jnp.float32
    )


def column_sums(got, comps, cells):
    slots, height, soundings = got.shape
    return pl.pallas_call(
        lambda *refs: gather_kernel(comps, *refs),
        out_shape=jax.ShapeDtypeStruct((height, cells), jnp.float32),
        grid=(slots // GROUP,),
        in_specs=[pl.BlockSpec((GROUP, height, soundings), lambda i: (i, 0, 0))],
        out_specs=pl.BlockSpec((height, cells), lambda i: (0, 0)),
        compiler_params=pltpu.CompilerParams(vmem_limit_bytes=32 * 2**20),
    )(got)


def per_device(control, kappa, pc_obs, owner, columns, counts, jacobian, obs_weight):
    peers = lax.axis_size("lat") * lax.axis_size("lon")
    fields, levels, rows, width_dev = control.shape
    blocks, soundings, comps = pc_obs.shape
    cells = rows * width_dev
    height = -(-(comps + 3) // 16) * 16
    slots = peers * CAP
    target = owner[:, 0]
    index = jnp.arange(blocks, dtype=jnp.int32)
    same = (target[:, None] == target[None, :]) & (index[None, :] < index[:, None])
    position = target * CAP + jnp.sum(same.astype(jnp.int32), axis=1)
    hits = position[None, :] == jnp.arange(slots, dtype=jnp.int32)[:, None]
    source = jnp.sum(jnp.where(hits, index[None, :], 0), axis=1)
    order = jnp.arange(soundings, dtype=jnp.int32)
    code = jnp.where(order[None, :] < counts[:, None], columns, -32)
    code = -32 + jnp.sum(jnp.where(hits[:, :, None], code[None] + 32, 0), axis=1)
    sent = pack(pc_obs, source, code, height)
    planes = fields * levels
    extent = rows + 2 * STEPS
    start = control.reshape(planes, rows, width_dev)
    field, side = rims(start, False)
    coef, coef_side = rims(kappa.reshape(planes, rows, width_dev), True)
    sent, side, coef_side = lax.optimization_barrier((sent, side, coef_side))
    got = lax.all_to_all(sent, ("lat", "lon"), split_axis=0, concat_axis=0, tiled=True)
    coef_side = strips(coef, coef_side, fields)
    state = spread(field, strips(field, side, fields), coef, coef_side, rows)
    table = state.astype(jnp.bfloat16).reshape(planes, cells)
    model = lax.dot_general(
        jacobian, table, (((0,), (0,)), ((), ())), preferred_element_type=jnp.float32
    )
    sums = column_sums(got, comps, cells)
    total = (sums[comps : comps + 1] * model - sums[:comps]) * obs_weight[:, None]
    total = total.astype(jnp.bfloat16).reshape(comps, rows, width_dev)
    total, total_side = rims(total, False)
    back, back_side = (
        lax.dot_general(
            jacobian, part.reshape(comps, -1), (((1,), (0,)), ((), ())), preferred_element_type=jnp.float32
        )
        for part in (total, total_side)
    )
    back = back.reshape(planes, extent, width_dev)
    return spread(back, strips(back, back_side, fields), coef, coef_side, rows, control)


def solution(mesh):
    placed = (
        P(None, None, "lat", "lon"),
        P(None, None, "lat", "lon"),
        P(("lat", "lon"), None, None),
        P(("lat", "lon"), None),
        P(("lat", "lon"), None),
        P(("lat", "lon")),
        P(),
        P(),
    )
    return jax.shard_map(
        per_device,
        mesh=mesh,
        in_specs=placed,
        out_specs=P(None, None, "lat", "lon"),
        check_vma=False,
    )
```

```python
import jax
import jax.numpy as jnp
from jax import lax
from jax.experimental import pallas as pl
from jax.experimental.pallas import tpu as pltpu
from jax.sharding import PartitionSpec as P

CAP = 2
STEPS = 4
GROUP = 4


def ring(axis, step):
    count = lax.axis_size(axis)
    return [(i, (i + step) % count) for i in range(count)]


def rims(core, closed):
    north = lax.ppermute(core[:, -STEPS:], "lat", ring("lat", 1))
    south = lax.ppermute(core[:, :STEPS], "lat", ring("lat", -1))
    if closed:
        place = lax.axis_index("lat")
        zero = jnp.zeros((), core.dtype)
        north = jnp.where(place == 0, zero, north)
        south = jnp.where(place == lax.axis_size("lat") - 1, zero, south)
    main = jnp.concatenate([core, south, north], axis=1)
    planes = main.shape[0]
    head = main[:, :, :STEPS].reshape(planes, -1)
    tail = main[:, :, -STEPS:].reshape(planes, -1)
    west = lax.ppermute(tail, "lon", ring("lon", 1))
    east = lax.ppermute(head, "lon", ring("lon", -1))
    return main, jnp.concatenate([east, west], axis=1)


def strips(main, side, fields):
    planes, rows, width = main.shape
    levels, near = planes // fields, 3 * STEPS
    body = main.reshape(fields, levels, rows, width)
    flat = side.reshape(fields, levels, 2, rows, STEPS)
    pieces = []
    for f in range(fields):
        pieces += [flat[f, :, 1], body[f, :, :, :near], body[f, :, :, width - near :], flat[f, :, 0]]
    return jnp.concatenate(pieces, axis=2)


def diffused(tiles, coefs):
    rows, lanes = tiles[0].shape
    south = [c * pltpu.roll(c, rows - 1, 0) for c in coefs]
    east = [c * pltpu.roll(c, lanes - 1, 1) for c in coefs]
    for repeat in range(STEPS):
        below = [pltpu.roll(t, rows - 1, 0) for t in tiles]
        beside = [pltpu.roll(t, lanes - 1, 1) for t in tiles]
        down = [w * (n - t) for w, n, t in zip(south, below, tiles)]
        along = [w * (n - t) for w, n, t in zip(east, beside, tiles)]
        up = [pltpu.roll(d, 1, 0) for d in down]
        back = [pltpu.roll(d, 1, 1) for d in along]
        tiles = [t + (d - u) + (g - h) for t, d, u, g, h in zip(tiles, down, up, along, back)]
    return tiles


def spread_kernel(field_ref, strip_ref, coef_ref, coef_strip_ref, *refs):
    out_ref = refs[-1]
    fields, levels, core, width = out_ref.shape
    slot = 8 * STEPS
    lane = lax.broadcasted_iota(jnp.int32, (core, width), 1)

    @pl.loop(0, levels)
    def _(i):
        tiles = [strip_ref[i]] + [field_ref[f, i] for f in range(fields)]
        coefs = [coef_strip_ref[i]] + [coef_ref[f, i] for f in range(fields)]
        added = [refs[0][f, i] for f in range(fields)] if len(refs) > 1 else None
        edge, *results = [t[:core] for t in diffused(tiles, coefs)]
        for f in range(fields):
            west = pltpu.roll(edge, (width - slot * f - STEPS) % width, 1)
            east = pltpu.roll(edge, (width - slot * f - slot + STEPS) % width, 1)
            results[f] = jnp.where(lane < STEPS, west, results[f])
            results[f] = jnp.where(lane >= width - STEPS, east, results[f])
            if added:
                results[f] = results[f] + added[f]
        for f in range(fields):
            out_ref[f, i] = results[f]


def spread(field, strip, coef, coef_strip, core, *base):
    planes, rows, width = field.shape
    levels = strip.shape[0]
    fields = planes // levels
    batch = max(n for n in range(1, 11) if levels % n == 0)
    wide = pl.BlockSpec((fields, batch, rows, width), lambda i: (0, i, 0, 0))
    edge = pl.BlockSpec((batch, rows, strip.shape[2]), lambda i: (i, 0, 0))
    thin = pl.BlockSpec((fields, batch, core, width), lambda i: (0, i, 0, 0))
    shape = (fields, levels, rows, width)
    return pl.pallas_call(
        spread_kernel,
        out_shape=jax.ShapeDtypeStruct((fields, levels, core, width), jnp.float32),
        grid=(levels // batch,),
        in_specs=[wide, edge, wide, edge] + [thin] * len(base),
        out_specs=thin,
        cost_estimate=pl.CostEstimate(
            flops=planes * rows * width * 50, bytes_accessed=planes * rows * width * 14, transcendentals=0
        ),
    )(field.reshape(shape), strip, coef.reshape(shape), coef_strip, *base)


def pack_kernel(source_ref, *refs):
    blocks, (code_ref, out_ref, wide) = refs[:CAP], refs[CAP:]
    comps = blocks[0].shape[2]
    for k, block in enumerate(blocks):
        wide[0:comps, :] = jnp.transpose(block[0].astype(jnp.float32))
        code = code_ref[0, k : k + 1, :]
        low = jnp.bitwise_and(code, 31)
        wide[comps : comps + 1, :] = jnp.ones((1, wide.shape[1]), jnp.float32)
        wide[comps + 1 : comps + 2, :] = jnp.right_shift(code - low, 5).astype(jnp.float32)
        wide[comps + 2 : comps + 3, :] = low.astype(jnp.float32)
        wide[comps + 3 :, :] = jnp.zeros((wide.shape[0] - comps - 3, wide.shape[1]), jnp.float32)
        out_ref[k] = wide[...].astype(jnp.bfloat16)


def pack(pc_obs, source, code, height):
    blocks, soundings, comps = pc_obs.shape
    slots = code.shape[0]

    def place(k):
        return lambda i, src: (src[i * CAP + k], 0, 0)

    return pl.pallas_call(
        pack_kernel,
        out_shape=jax.ShapeDtypeStruct((slots, height, soundings), jnp.bfloat16),
        grid_spec=pltpu.PrefetchScalarGridSpec(
            num_scalar_prefetch=1,
            grid=(slots // CAP,),
            in_specs=[pl.BlockSpec((1, soundings, comps), place(k)) for k in range(CAP)]
            + [pl.BlockSpec((1, CAP, soundings), lambda i, src: (i, 0, 0))],
            out_specs=pl.BlockSpec((CAP, height, soundings), lambda i, src: (i, 0, 0)),
            scratch_shapes=[pltpu.VMEM((height, soundings), jnp.float32)],
        ),
    )(source, *([pc_obs] * CAP), code.reshape(slots // CAP, CAP, soundings))


def gather_kernel(comps, got_ref, sums_ref):
    height, cells = sums_ref.shape

    @pl.when(pl.program_id(0) == 0)
    def _():
        sums_ref[...] = jnp.zeros_like(sums_ref)

    base = height - 16
    lines = []
    for k in range(GROUP):
        tail = got_ref[k, base:height, :].astype(jnp.float32)
        high = tail[comps + 1 - base : comps + 2 - base, :]
        lines.append((high * 32.0 + tail[comps + 2 - base : comps + 3 - base, :]).astype(jnp.int32))
    code = jnp.concatenate(lines, axis=1)
    cell = lax.broadcasted_iota(jnp.int32, (cells, code.shape[1]), 0)
    hot = jnp.where(cell == code, 1.0, 0.0).astype(jnp.bfloat16)
    obs = jnp.concatenate([got_ref[k] for k in range(GROUP)], axis=1)
    sums_ref[...] += lax.dot_general(
        obs, hot, (((1,), (1,)), ((), ())), preferred_element_type=jnp.float32
    )


def column_sums(got, comps, cells):
    slots, height, soundings = got.shape
    return pl.pallas_call(
        lambda *refs: gather_kernel(comps, *refs),
        out_shape=jax.ShapeDtypeStruct((height, cells), jnp.float32),
        grid=(slots // GROUP,),
        in_specs=[pl.BlockSpec((GROUP, height, soundings), lambda i: (i, 0, 0))],
        out_specs=pl.BlockSpec((height, cells), lambda i: (0, 0)),
        compiler_params=pltpu.CompilerParams(vmem_limit_bytes=32 * 2**20),
    )(got)


def per_device(control, kappa, pc_obs, owner, columns, counts, jacobian, obs_weight):
    peers = lax.axis_size("lat") * lax.axis_size("lon")
    fields, levels, rows, width_dev = control.shape
    blocks, soundings, comps = pc_obs.shape
    cells = rows * width_dev
    height = -(-(comps + 3) // 16) * 16
    slots = peers * CAP
    target = owner[:, 0]
    index = jnp.arange(blocks, dtype=jnp.int32)
    same = (target[:, None] == target[None, :]) & (index[None, :] < index[:, None])
    position = target * CAP + jnp.sum(same.astype(jnp.int32), axis=1)
    hits = position[None, :] == jnp.arange(slots, dtype=jnp.int32)[:, None]
    source = jnp.sum(jnp.where(hits, index[None, :], 0), axis=1)
    order = jnp.arange(soundings, dtype=jnp.int32)
    code = jnp.where(order[None, :] < counts[:, None], columns, -32)
    code = -32 + jnp.sum(jnp.where(hits[:, :, None], code[None] + 32, 0), axis=1)
    sent = pack(pc_obs, source, code, height)
    planes = fields * levels
    extent = rows + 2 * STEPS
    start = control.reshape(planes, rows, width_dev)
    field, side = rims(start, False)
    coef, coef_side = rims(kappa.reshape(planes, rows, width_dev), True)
    sent, side, coef_side = lax.optimization_barrier((sent, side, coef_side))
    got = lax.all_to_all(sent, ("lat", "lon"), split_axis=0, concat_axis=0, tiled=True)
    coef_side = strips(coef, coef_side, fields)
    state = spread(field, strips(field, side, fields), coef, coef_side, rows)
    table = state.astype(jnp.bfloat16).reshape(planes, cells)
    model = lax.dot_general(
        jacobian, table, (((0,), (0,)), ((), ())), preferred_element_type=jnp.float32
    )
    sums = column_sums(got, comps, cells)
    total = (sums[comps : comps + 1] * model - sums[:comps]) * obs_weight[:, None]
    total = total.astype(jnp.bfloat16).reshape(comps, rows, width_dev)
    total, total_side = rims(total, False)
    back, back_side = (
        lax.dot_general(
            jacobian, part.reshape(comps, -1), (((1,), (0,)), ((), ())), preferred_element_type=jnp.float32
        )
        for part in (total, total_side)
    )
    back = back.reshape(planes, extent, width_dev)
    return spread(back, strips(back, back_side, fields), coef, coef_side, rows, control)


def solution(mesh):
    placed = (
        P(None, None, "lat", "lon"),
        P(None, None, "lat", "lon"),
        P(("lat", "lon"), None, None),
        P(("lat", "lon"), None),
        P(("lat", "lon"), None),
        P(("lat", "lon")),
        P(),
        P(),
    )
    return jax.shard_map(
        per_device,
        mesh=mesh,
        in_specs=placed,
        out_specs=P(None, None, "lat", "lon"),
        check_vma=False,
    )
```

```python
import jax
import jax.numpy as jnp
from jax import lax
from jax.experimental import pallas as pl
from jax.experimental.pallas import tpu as pltpu
from jax.sharding import PartitionSpec as P

CAP = 2
STEPS = 4
GROUP = 4


def ring(axis, step):
    count = lax.axis_size(axis)
    return [(i, (i + step) % count) for i in range(count)]


def rims(core, closed):
    north = lax.ppermute(core[:, -STEPS:].astype(jnp.bfloat16), "lat", ring("lat", 1)).astype(core.dtype)
    south = lax.ppermute(core[:, :STEPS].astype(jnp.bfloat16), "lat", ring("lat", -1)).astype(core.dtype)
    if closed:
        place = lax.axis_index("lat")
        zero = jnp.zeros((), core.dtype)
        north = jnp.where(place == 0, zero, north)
        south = jnp.where(place == lax.axis_size("lat") - 1, zero, south)
    main = jnp.concatenate([core, south, north], axis=1)
    planes = main.shape[0]
    head = main[:, :, :STEPS].reshape(planes, -1).astype(jnp.bfloat16)
    tail = main[:, :, -STEPS:].reshape(planes, -1).astype(jnp.bfloat16)
    west = lax.ppermute(tail, "lon", ring("lon", 1))
    east = lax.ppermute(head, "lon", ring("lon", -1))
    return main, jnp.concatenate([east, west], axis=1).astype(core.dtype)


def side_tile(side, rows, width):
    planes = side.shape[0]
    parts = side.reshape(planes, 2, rows, STEPS)
    gap = jnp.zeros((planes, rows, width - 2 * STEPS), side.dtype)
    return jnp.concatenate([parts[:, 0], gap, parts[:, 1]], axis=2)


def spread_kernel(field_ref, side_ref, coef_ref, coef_side_ref, *refs):
    out_ref = refs[-1]
    core, width = out_ref.shape[1:]
    rows, lanes = field_ref.shape[1], 2 * width

    @pl.loop(0, out_ref.shape[0], unroll=4)
    def _(i):
        coef = jnp.concatenate([coef_ref[i], coef_side_ref[i]], axis=1)
        field = jnp.concatenate([field_ref[i], side_ref[i]], axis=1)
        south = coef * pltpu.roll(coef, rows - 1, 0)
        east = coef * pltpu.roll(coef, lanes - 1, 1)
        for repeat in range(STEPS):
            down = south * (pltpu.roll(field, rows - 1, 0) - field)
            along = east * (pltpu.roll(field, lanes - 1, 1) - field)
            field = field + (down - pltpu.roll(down, 1, 0)) + (along - pltpu.roll(along, 1, 1))
        result = field[:core, :width]
        out_ref[i] = result + refs[0][i] if len(refs) > 1 else result


def spread(field, side, coef, coef_side, core, *base):
    planes, rows, width = field.shape
    batch = max(n for n in range(4, 41, 4) if planes % n == 0)
    wide = pl.BlockSpec((batch, rows, width), lambda i: (i, 0, 0))
    thin = pl.BlockSpec((batch, core, width), lambda i: (i, 0, 0))
    return pl.pallas_call(
        spread_kernel,
        out_shape=jax.ShapeDtypeStruct((planes, core, width), jnp.float32),
        grid=(planes // batch,),
        in_specs=[wide] * 4 + [thin] * len(base),
        out_specs=thin,
        cost_estimate=pl.CostEstimate(
            flops=planes * rows * width * 80, bytes_accessed=planes * rows * width * 20, transcendentals=0
        ),
    )(field, side, coef, coef_side, *base)


def pack_kernel(source_ref, *refs):
    blocks, (code_ref, out_ref, wide) = refs[:CAP], refs[CAP:]
    comps = blocks[0].shape[2]
    for k, block in enumerate(blocks):
        wide[0:comps, :] = jnp.transpose(block[0].astype(jnp.float32))
        code = code_ref[0, k : k + 1, :]
        low = jnp.bitwise_and(code, 31)
        wide[comps : comps + 1, :] = jnp.ones((1, wide.shape[1]), jnp.float32)
        wide[comps + 1 : comps + 2, :] = jnp.right_shift(code - low, 5).astype(jnp.float32)
        wide[comps + 2 : comps + 3, :] = low.astype(jnp.float32)
        wide[comps + 3 :, :] = jnp.zeros((wide.shape[0] - comps - 3, wide.shape[1]), jnp.float32)
        out_ref[k] = wide[...].astype(jnp.bfloat16)


def pack(pc_obs, source, code, height):
    blocks, soundings, comps = pc_obs.shape
    slots = code.shape[0]

    def place(k):
        return lambda i, src: (src[i * CAP + k], 0, 0)

    return pl.pallas_call(
        pack_kernel,
        out_shape=jax.ShapeDtypeStruct((slots, height, soundings), jnp.bfloat16),
        grid_spec=pltpu.PrefetchScalarGridSpec(
            num_scalar_prefetch=1,
            grid=(slots // CAP,),
            in_specs=[pl.BlockSpec((1, soundings, comps), place(k)) for k in range(CAP)]
            + [pl.BlockSpec((1, CAP, soundings), lambda i, src: (i, 0, 0))],
            out_specs=pl.BlockSpec((CAP, height, soundings), lambda i, src: (i, 0, 0)),
            scratch_shapes=[pltpu.VMEM((height, soundings), jnp.float32)],
        ),
    )(source, *([pc_obs] * CAP), code.reshape(slots // CAP, CAP, soundings))


def gather_kernel(comps, got_ref, sums_ref):
    height, cells = sums_ref.shape

    @pl.when(pl.program_id(0) == 0)
    def _():
        sums_ref[...] = jnp.zeros_like(sums_ref)

    base = height - 16
    lines = []
    for k in range(GROUP):
        tail = got_ref[k, base:height, :].astype(jnp.float32)
        high = tail[comps + 1 - base : comps + 2 - base, :]
        lines.append((high * 32.0 + tail[comps + 2 - base : comps + 3 - base, :]).astype(jnp.int32))
    code = jnp.concatenate(lines, axis=1)
    cell = lax.broadcasted_iota(jnp.int32, (cells, code.shape[1]), 0)
    hot = jnp.where(cell == code, 1.0, 0.0).astype(jnp.bfloat16)
    obs = jnp.concatenate([got_ref[k] for k in range(GROUP)], axis=1)
    sums_ref[...] += lax.dot_general(
        obs, hot, (((1,), (1,)), ((), ())), preferred_element_type=jnp.float32
    )


def column_sums(got, comps, cells):
    slots, height, soundings = got.shape
    return pl.pallas_call(
        lambda *refs: gather_kernel(comps, *refs),
        out_shape=jax.ShapeDtypeStruct((height, cells), jnp.float32),
        grid=(slots // GROUP,),
        in_specs=[pl.BlockSpec((GROUP, height, soundings), lambda i: (i, 0, 0))],
        out_specs=pl.BlockSpec((height, cells), lambda i: (0, 0)),
        compiler_params=pltpu.CompilerParams(vmem_limit_bytes=32 * 2**20),
    )(got)


def per_device(control, kappa, pc_obs, owner, columns, counts, jacobian, obs_weight):
    peers = lax.axis_size("lat") * lax.axis_size("lon")
    fields, levels, rows, width_dev = control.shape
    blocks, soundings, comps = pc_obs.shape
    cells = rows * width_dev
    height = -(-(comps + 3) // 16) * 16
    slots = peers * CAP
    target = owner[:, 0]
    index = jnp.arange(blocks, dtype=jnp.int32)
    same = (target[:, None] == target[None, :]) & (index[None, :] < index[:, None])
    position = target * CAP + jnp.sum(same.astype(jnp.int32), axis=1)
    hits = position[None, :] == jnp.arange(slots, dtype=jnp.int32)[:, None]
    source = jnp.sum(jnp.where(hits, index[None, :], 0), axis=1)
    order = jnp.arange(soundings, dtype=jnp.int32)
    code = jnp.where(order[None, :] < counts[:, None], columns, -32)
    code = -32 + jnp.sum(jnp.where(hits[:, :, None], code[None] + 32, 0), axis=1)
    sent = pack(pc_obs, source, code, height)
    planes = fields * levels
    extent = rows + 2 * STEPS
    start = control.reshape(planes, rows, width_dev)
    field, side = rims(start, False)
    coef, coef_side = rims(kappa.reshape(planes, rows, width_dev), True)
    sent, side, coef_side = lax.optimization_barrier((sent, side, coef_side))
    got = lax.all_to_all(sent, ("lat", "lon"), split_axis=0, concat_axis=0, tiled=True)
    coef_side = side_tile(coef_side, extent, width_dev)
    state = spread(field, side_tile(side, extent, width_dev), coef, coef_side, rows)
    table = state.astype(jnp.bfloat16).reshape(planes, cells)
    model = lax.dot_general(
        jacobian, table, (((0,), (0,)), ((), ())), preferred_element_type=jnp.float32
    )
    sums = column_sums(got, comps, cells)
    total = (sums[comps : comps + 1] * model - sums[:comps]) * obs_weight[:, None]
    total = total.astype(jnp.bfloat16).reshape(comps, rows, width_dev)
    total, total_side = rims(total, False)
    back, back_side = (
        lax.dot_general(
            jacobian, part.reshape(comps, -1), (((1,), (0,)), ((), ())), preferred_element_type=jnp.float32
        )
        for part in (total, total_side)
    )
    back = back.reshape(planes, extent, width_dev)
    result = spread(back, side_tile(back_side, extent, width_dev), coef, coef_side, rows, start)
    return result.reshape(control.shape)


def solution(mesh):
    placed = (
        P(None, None, "lat", "lon"),
        P(None, None, "lat", "lon"),
        P(("lat", "lon"), None, None),
        P(("lat", "lon"), None),
        P(("lat", "lon"), None),
        P(("lat", "lon")),
        P(),
        P(),
    )
    return jax.shard_map(
        per_device,
        mesh=mesh,
        in_specs=placed,
        out_specs=P(None, None, "lat", "lon"),
        check_vma=False,
    )
```

```python
import jax
import jax.numpy as jnp
from jax import lax
from jax.experimental import pallas as pl
from jax.experimental.pallas import tpu as pltpu
from jax.sharding import PartitionSpec as P

CAP = 2
STEPS = 4
GROUP = 4


def ring(axis, step):
    count = lax.axis_size(axis)
    return [(i, (i + step) % count) for i in range(count)]


def rims(core, closed):
    north = lax.ppermute(core[:, -STEPS:].astype(jnp.bfloat16), "lat", ring("lat", 1)).astype(core.dtype)
    south = lax.ppermute(core[:, :STEPS].astype(jnp.bfloat16), "lat", ring("lat", -1)).astype(core.dtype)
    if closed:
        place = lax.axis_index("lat")
        zero = jnp.zeros((), core.dtype)
        north = jnp.where(place == 0, zero, north)
        south = jnp.where(place == lax.axis_size("lat") - 1, zero, south)
    main = jnp.concatenate([core, south, north], axis=1)
    planes = main.shape[0]
    head = main[:, :, :STEPS].reshape(planes, -1).astype(jnp.bfloat16)
    tail = main[:, :, -STEPS:].reshape(planes, -1).astype(jnp.bfloat16)
    west = lax.ppermute(tail, "lon", ring("lon", 1))
    east = lax.ppermute(head, "lon", ring("lon", -1))
    return main, jnp.concatenate([east, west], axis=1).astype(core.dtype)


def side_tile(side, rows, width):
    planes = side.shape[0]
    parts = side.reshape(planes, 2, rows, STEPS)
    gap = jnp.zeros((planes, rows, width - 2 * STEPS), side.dtype)
    return jnp.concatenate([parts[:, 0], gap, parts[:, 1]], axis=2)


def spread_kernel(field_ref, side_ref, coef_ref, coef_side_ref, *refs):
    out_ref = refs[-1]
    core, width = out_ref.shape[1:]
    rows, lanes = field_ref.shape[1], 2 * width

    @pl.loop(0, out_ref.shape[0], unroll=8)
    def _(i):
        coef = jnp.concatenate([coef_ref[i], coef_side_ref[i]], axis=1)
        field = jnp.concatenate([field_ref[i], side_ref[i]], axis=1)
        south = coef * pltpu.roll(coef, rows - 1, 0)
        east = coef * pltpu.roll(coef, lanes - 1, 1)
        for repeat in range(STEPS):
            down = south * (pltpu.roll(field, rows - 1, 0) - field)
            along = east * (pltpu.roll(field, lanes - 1, 1) - field)
            field = field + (down - pltpu.roll(down, 1, 0)) + (along - pltpu.roll(along, 1, 1))
        result = field[:core, :width]
        out_ref[i] = result + refs[0][i] if len(refs) > 1 else result


def spread(field, side, coef, coef_side, core, *base):
    planes, rows, width = field.shape
    batch = max(n for n in range(4, 41, 4) if planes % n == 0)
    wide = pl.BlockSpec((batch, rows, width), lambda i: (i, 0, 0))
    thin = pl.BlockSpec((batch, core, width), lambda i: (i, 0, 0))
    return pl.pallas_call(
        spread_kernel,
        out_shape=jax.ShapeDtypeStruct((planes, core, width), jnp.float32),
        grid=(planes // batch,),
        in_specs=[wide] * 4 + [thin] * len(base),
        out_specs=thin,
        cost_estimate=pl.CostEstimate(
            flops=planes * rows * width * 80, bytes_accessed=planes * rows * width * 20, transcendentals=0
        ),
    )(field, side, coef, coef_side, *base)


def pack_kernel(source_ref, *refs):
    blocks, (code_ref, out_ref, wide) = refs[:CAP], refs[CAP:]
    comps = blocks[0].shape[2]
    for k, block in enumerate(blocks):
        wide[0:comps, :] = jnp.transpose(block[0].astype(jnp.float32))
        code = code_ref[0, k : k + 1, :]
        low = jnp.bitwise_and(code, 31)
        wide[comps : comps + 1, :] = jnp.ones((1, wide.shape[1]), jnp.float32)
        wide[comps + 1 : comps + 2, :] = jnp.right_shift(code - low, 5).astype(jnp.float32)
        wide[comps + 2 : comps + 3, :] = low.astype(jnp.float32)
        wide[comps + 3 :, :] = jnp.zeros((wide.shape[0] - comps - 3, wide.shape[1]), jnp.float32)
        out_ref[k] = wide[...].astype(jnp.bfloat16)


def pack(pc_obs, source, code, height):
    blocks, soundings, comps = pc_obs.shape
    slots = code.shape[0]

    def place(k):
        return lambda i, src: (src[i * CAP + k], 0, 0)

    return pl.pallas_call(
        pack_kernel,
        out_shape=jax.ShapeDtypeStruct((slots, height, soundings), jnp.bfloat16),
        grid_spec=pltpu.PrefetchScalarGridSpec(
            num_scalar_prefetch=1,
            grid=(slots // CAP,),
            in_specs=[pl.BlockSpec((1, soundings, comps), place(k)) for k in range(CAP)]
            + [pl.BlockSpec((1, CAP, soundings), lambda i, src: (i, 0, 0))],
            out_specs=pl.BlockSpec((CAP, height, soundings), lambda i, src: (i, 0, 0)),
            scratch_shapes=[pltpu.VMEM((height, soundings), jnp.float32)],
        ),
    )(source, *([pc_obs] * CAP), code.reshape(slots // CAP, CAP, soundings))


def gather_kernel(comps, got_ref, sums_ref):
    height, cells = sums_ref.shape

    @pl.when(pl.program_id(0) == 0)
    def _():
        sums_ref[...] = jnp.zeros_like(sums_ref)

    base = height - 16
    lines = []
    for k in range(GROUP):
        tail = got_ref[k, base:height, :].astype(jnp.float32)
        high = tail[comps + 1 - base : comps + 2 - base, :]
        lines.append((high * 32.0 + tail[comps + 2 - base : comps + 3 - base, :]).astype(jnp.int32))
    code = jnp.concatenate(lines, axis=1)
    cell = lax.broadcasted_iota(jnp.int32, (cells, code.shape[1]), 0)
    hot = jnp.where(cell == code, 1.0, 0.0).astype(jnp.bfloat16)
    obs = jnp.concatenate([got_ref[k] for k in range(GROUP)], axis=1)
    sums_ref[...] += lax.dot_general(
        obs, hot, (((1,), (1,)), ((), ())), preferred_element_type=jnp.float32
    )


def column_sums(got, comps, cells):
    slots, height, soundings = got.shape
    return pl.pallas_call(
        lambda *refs: gather_kernel(comps, *refs),
        out_shape=jax.ShapeDtypeStruct((height, cells), jnp.float32),
        grid=(slots // GROUP,),
        in_specs=[pl.BlockSpec((GROUP, height, soundings), lambda i: (i, 0, 0))],
        out_specs=pl.BlockSpec((height, cells), lambda i: (0, 0)),
        compiler_params=pltpu.CompilerParams(vmem_limit_bytes=32 * 2**20),
    )(got)


def per_device(control, kappa, pc_obs, owner, columns, counts, jacobian, obs_weight):
    peers = lax.axis_size("lat") * lax.axis_size("lon")
    fields, levels, rows, width_dev = control.shape
    blocks, soundings, comps = pc_obs.shape
    cells = rows * width_dev
    height = -(-(comps + 3) // 16) * 16
    slots = peers * CAP
    target = owner[:, 0]
    index = jnp.arange(blocks, dtype=jnp.int32)
    same = (target[:, None] == target[None, :]) & (index[None, :] < index[:, None])
    position = target * CAP + jnp.sum(same.astype(jnp.int32), axis=1)
    hits = position[None, :] == jnp.arange(slots, dtype=jnp.int32)[:, None]
    source = jnp.sum(jnp.where(hits, index[None, :], 0), axis=1)
    order = jnp.arange(soundings, dtype=jnp.int32)
    code = jnp.where(order[None, :] < counts[:, None], columns, -32)
    code = -32 + jnp.sum(jnp.where(hits[:, :, None], code[None] + 32, 0), axis=1)
    sent = pack(pc_obs, source, code, height)
    planes = fields * levels
    extent = rows + 2 * STEPS
    start = control.reshape(planes, rows, width_dev)
    field, side = rims(start, False)
    coef, coef_side = rims(kappa.reshape(planes, rows, width_dev), True)
    sent, side, coef_side = lax.optimization_barrier((sent, side, coef_side))
    got = lax.all_to_all(sent, ("lat", "lon"), split_axis=0, concat_axis=0, tiled=True)
    coef_side = side_tile(coef_side, extent, width_dev)
    state = spread(field, side_tile(side, extent, width_dev), coef, coef_side, rows)
    table = state.astype(jnp.bfloat16).reshape(planes, cells)
    model = lax.dot_general(
        jacobian, table, (((0,), (0,)), ((), ())), preferred_element_type=jnp.float32
    )
    sums = column_sums(got, comps, cells)
    total = (sums[comps : comps + 1] * model - sums[:comps]) * obs_weight[:, None]
    total = total.astype(jnp.bfloat16).reshape(comps, rows, width_dev)
    total, total_side = rims(total, False)
    back, back_side = (
        lax.dot_general(
            jacobian, part.reshape(comps, -1), (((1,), (0,)), ((), ())), preferred_element_type=jnp.float32
        )
        for part in (total, total_side)
    )
    back = back.reshape(planes, extent, width_dev)
    result = spread(back, side_tile(back_side, extent, width_dev), coef, coef_side, rows, start)
    return result.reshape(control.shape)


def solution(mesh):
    placed = (
        P(None, None, "lat", "lon"),
        P(None, None, "lat", "lon"),
        P(("lat", "lon"), None, None),
        P(("lat", "lon"), None),
        P(("lat", "lon"), None),
        P(("lat", "lon")),
        P(),
        P(),
    )
    return jax.shard_map(
        per_device,
        mesh=mesh,
        in_specs=placed,
        out_specs=P(None, None, "lat", "lon"),
        check_vma=False,
    )
```
